128 devices in a mesh: row: 16 (over x_hi, y, core), col: 8 (over x_lo, z).
Axes of the slice: x: 4 (x_hi: 2, x_lo: 2; x = x_hi * 2 + x_lo), y: 4, z: 4, core: 2. Of those that a mesh axis runs over, the one named last changes fastest.
Arguments:
- tokens: bfloat16 [1024, 12288], P('row', 'col'), may hold values from -6 to 6
- in_weight: bfloat16 [12288, 24576], P('col', 'row'), may hold values from -0.0546875 to 0.0546875
- in_bias: float32 [24576], P('row'), may hold values from -3 to 3
- out_weight: bfloat16 [24576, 12288], P('row', 'col'), may hold values from -0.0390625 to 0.0390625
- out_bias: float32 [12288], P('col'), may hold values from -3 to 3
- out_grad: bfloat16 [1024, 12288], P('row', 'col'), may hold values from -6 to 6
Outputs:
- output: float32 [1024, 12288], P('row', 'col')
- grad_tokens: float32 [1024, 12288], P('row', 'col')
- grad_in_weight: bfloat16 [12288, 24576], P('col', 'row')
- grad_in_bias: float32 [24576], P('row')
- grad_out_weight: float32 [24576, 12288], P('row', 'col')
- grad_out_bias: float32 [12288], P('col')
The draws below stay inside these ranges and needn't reach their ends.
All inputs are finite; a program needn't handle non-finite values.
Results may differ from the reference program's by a relative error of at most 0.0049.
Values may be sent and summed in bfloat16 or wider, within the bound.
No kernel may reach another device: no remote copies, remote signals or barrier semaphores. Data moves between devices by JAX's collectives and lax.ppermute only.
A program may use at most 128 MiB of HBM per device.

```python
import jax
import jax.numpy as jnp
from jax import lax

D = 12288
FF = 24576
TOKENS = 1024


def steps_of(rng, shape, split, smallest, largest):
    def one(dim, parts):
        steps = jax.random.uniform(jax.random.fold_in(jax.random.fold_in(rng, 6), dim), (parts,), jnp.float32, smallest / len(split), largest / len(split))
        return jnp.repeat(jnp.exp(steps), shape[dim] // parts).reshape((-1,) + (1,) * (len(shape) - dim - 1))

    level = one(*split[0])
    for cut in split[1:]:
        level = level * one(*cut)
    return level


def gaussian(stream_key, extent, deviation, bound, pieces=(), held_as=jnp.bfloat16):
    result = jax.random.normal(stream_key, extent, jnp.float32) * deviation
    if len(pieces) > 0:
        result = steps_of(stream_key, extent, pieces, -0.22, 0.18) * result
    return jnp.clip(result, min=-bound, max=bound).astype(held_as)


def setup_inputs(seed: int = 0) -> dict:
    keys = jax.random.split(jax.random.key(seed), 7)
    return {
        "tokens": gaussian(keys[0], (TOKENS, D), 1.0, 6.0, ((0, 16), (1, 8))),
        "in_weight": gaussian(keys[1], (D, FF), D ** -0.5, 0.0546875, ((0, 8), (1, 16))),
        "in_bias": gaussian(keys[2], (FF,), 0.5, 3.0, ((0, 16),), jnp.float32),
        "out_weight": gaussian(keys[3], (FF, D), FF ** -0.5, 0.0390625, ((0, 16), (1, 8))),
        "out_bias": gaussian(keys[4], (D,), 0.5, 3.0, ((0, 8),), jnp.float32),
        "out_grad": gaussian(keys[5], (TOKENS, D), 1.0, 6.0, ((0, 16), (1, 8))),
    }


def gelu_tanh(value):
    return jax.nn.gelu(value, approximate=True)

def reference(tokens, in_weight, in_bias, out_weight, out_bias, out_grad):
    pre_act = jnp.dot(tokens, in_weight, preferred_element_type=jnp.float32) + in_bias
    act = gelu_tanh(pre_act).astype(jnp.bfloat16)
    output = jnp.dot(act, out_weight, preferred_element_type=jnp.float32) + out_bias
    grad_act = lax.dot_general(out_grad, out_weight, (((1,), (1,)), ((), ())), preferred_element_type=jnp.float32)
    _, pull_back = jax.vjp(gelu_tanh, pre_act)
    grad_pre = pull_back(grad_act)[0].astype(jnp.bfloat16)
    grad_out_weight = lax.dot_general(act, out_grad, (((0,), (0,)), ((), ())), preferred_element_type=jnp.float32)
    grad_out_bias = lax.optimization_barrier(jnp.sum(out_grad, axis=0, dtype=jnp.float32))
    grad_in_weight = lax.dot_general(tokens, grad_pre, (((0,), (0,)), ((), ())), preferred_element_type=jnp.float32).astype(jnp.bfloat16)
    grad_in_bias = lax.optimization_barrier(jnp.sum(grad_pre, axis=0, dtype=jnp.float32))
    grad_tokens = lax.dot_general(grad_pre, in_weight, (((1,), (1,)), ((), ())), preferred_element_type=jnp.float32)
    return (output, grad_tokens, grad_in_weight, grad_in_bias, grad_out_weight, grad_out_bias)
```

```python
import jax
import jax.numpy as jnp
from jax import lax
from jax.sharding import PartitionSpec as P

BF = jnp.bfloat16
F32 = jnp.float32


def gelu_tanh(value):
    return jax.nn.gelu(value, approximate=True)


def contract_last(left, right):
    return lax.dot_general(left, right, (((1,), (1,)), ((), ())), preferred_element_type=F32)


def contract_first(left, right):
    return lax.dot_general(left, right, (((0,), (0,)), ((), ())), preferred_element_type=F32)


def matmul(left, right):
    return jnp.dot(left, right, preferred_element_type=F32)


def row_index(hi, y, core):
    return (hi * 4 + y) * 2 + core


def send_row(block, pair, step):
    perm = [
        (row_index(h, y, c), row_index(h ^ pair, (y + step) % 4, c))
        for h in range(2) for y in range(4) for c in range(2)
    ]
    return lax.ppermute(block, "row", perm)


def send_col(block, pair, step):
    perm = [(a * 4 + z, (a ^ pair) * 4 + (z + step) % 4) for a in range(2) for z in range(4)]
    return lax.ppermute(block, "col", perm)


def swap_core(block):
    return lax.ppermute(block, "row", [(i, i ^ 1) for i in range(16)])


def gather(own, send):
    half = own.shape[0] // 2
    before, after, pair = send(own, 0, 1), send(own, 0, -1), send(own, 1, 0)
    low, high = send(before[:half], 0, 1), send(after[half:], 0, -1)
    pair_before, pair_after = send(pair, 0, 1), send(pair, 0, -1)
    opposite = jnp.concatenate([low, high], axis=0)
    pair_opposite = send(opposite, 1, 0)
    return {
        (0, 0): own, (0, 1): after, (0, 2): opposite, (0, 3): before,
        (1, 0): pair, (1, 1): pair_after, (1, 2): pair_opposite, (1, 3): pair_before,
    }


def scatter(part, send):
    far = send(part(1, 2).astype(BF), 1, 0)
    from_before, from_after = send(part(1, 1).astype(BF), 0, 1), send(part(1, 3).astype(BF), 0, -1)
    opposite = part(0, 2) + far.astype(F32)
    half = opposite.shape[0] // 2
    low = send(opposite[:half].astype(BF), 0, 1)
    high = send(opposite[half:].astype(BF), 0, -1)
    pair = send((part(1, 0) + from_before.astype(F32) + from_after.astype(F32)).astype(BF), 1, 0)
    up, down = part(0, 1), part(0, 3)
    up = jnp.concatenate([up[:half] + low.astype(F32), up[half:]], axis=0)
    down = jnp.concatenate([down[:half], down[half:] + high.astype(F32)], axis=0)
    before, after = send(up.astype(BF), 0, 1), send(down.astype(BF), 0, -1)
    return part(0, 0) + pair.astype(F32) + before.astype(F32) + after.astype(F32)


ORDER = [(b, k) for b in range(2) for k in range(4)]


def row_panel(own):
    pieces = gather(own, send_row)
    mine = jnp.concatenate([pieces[s] for s in ORDER], axis=0)
    return jnp.concatenate([mine, swap_core(mine)], axis=0)


def row_share(half_term, rows):
    other = swap_core(half_term(1).astype(BF))
    mine = half_term(0) + other.astype(F32)

    def part(pair, step):
        at = (pair * 4 + step) * rows
        return mine[at:at + rows]

    return scatter(part, send_row)


def column_share(panel_term, rows):
    a, z = lax.axis_index("col") // 4, lax.axis_index("col") % 4
    far = panel_term((1 - a) * 4 * rows, 4 * rows)
    near = panel_term(a * 4 * rows, 4 * rows)

    def part(pair, step):
        at = ((z + step) % 4) * rows
        return lax.dynamic_slice_in_dim(far if pair else near, at, rows, 0)

    return scatter(part, send_col)


def column_panel(own):
    a, z = lax.axis_index("col") // 4, lax.axis_index("col") % 4
    pieces = gather(own, send_col)
    rows = own.shape[0]
    panel = jnp.zeros((8 * rows, own.shape[1]), own.dtype)
    for (pair, step), piece in pieces.items():
        at = ((a ^ pair) * 4 + (z + step) % 4) * rows
        panel = lax.dynamic_update_slice_in_dim(panel, piece, at, 0)
    return panel


def body(tokens, in_weight, in_bias, out_weight, out_bias, out_grad):
    rows = tokens.shape[0]
    tok_all = row_panel(tokens)
    grad_all = row_panel(out_grad)
    col_rows = tok_all.shape[0] // 8

    def hidden_term(start, count):
        return matmul(lax.dynamic_slice_in_dim(tok_all, start, count, 0), in_weight)

    def grad_act_term(start, count):
        return contract_last(lax.dynamic_slice_in_dim(grad_all, start, count, 0), out_weight)

    pre_act = column_share(hidden_term, col_rows) + in_bias
    grad_act = column_share(grad_act_term, col_rows)
    act = gelu_tanh(pre_act).astype(BF)
    act_all = column_panel(act)
    _, pull_back = jax.vjp(gelu_tanh, pre_act)
    grad_pre = pull_back(grad_act)[0].astype(BF)
    grad_pre_all = column_panel(grad_pre)

    def output_term(d):
        return matmul(act_all[d * 8 * rows:(d + 1) * 8 * rows], out_weight)

    def input_grad_term(d):
        return contract_last(grad_pre_all[d * 8 * rows:(d + 1) * 8 * rows], in_weight)

    output = row_share(output_term, rows) + out_bias
    grad_out_weight = contract_first(act_all, grad_all)
    grad_out_bias = jnp.sum(grad_all, axis=0, dtype=F32)
    grad_tokens = row_share(input_grad_term, rows)
    grad_in_weight = contract_first(tok_all, grad_pre_all).astype(BF)
    grad_in_bias = jnp.sum(grad_pre_all, axis=0, dtype=F32)
    return (output, grad_tokens, grad_in_weight, grad_in_bias, grad_out_weight, grad_out_bias)


def solution(mesh):
    in_specs = (
        P("row", "col"),
        P("col", "row"),
        P("row"),
        P("row", "col"),
        P("col"),
        P("row", "col"),
    )
    out_specs = (
        P("row", "col"),
        P("row", "col"),
        P("col", "row"),
        P("row"),
        P("row", "col"),
        P("col"),
    )
    return jax.shard_map(body, mesh=mesh, in_specs=in_specs, out_specs=out_specs, check_vma=False)
```

```python
import jax
import jax.numpy as jnp
from jax import lax
from jax.sharding import PartitionSpec as P

BF = jnp.bfloat16
F32 = jnp.float32


def gelu_tanh(value):
    return jax.nn.gelu(value, approximate=True)


def contract_last(left, right):
    return lax.dot_general(left, right, (((1,), (1,)), ((), ())), preferred_element_type=F32)


def contract_first(left, right):
    return lax.dot_general(left, right, (((0,), (0,)), ((), ())), preferred_element_type=F32)


def matmul(left, right):
    return jnp.dot(left, right, preferred_element_type=F32)


def row_index(hi, y, core):
    return (hi * 4 + y) * 2 + core


def send_row(block, pair, step):
    perm = [
        (row_index(h, y, c), row_index(h ^ pair, (y + step) % 4, c))
        for h in range(2) for y in range(4) for c in range(2)
    ]
    return lax.ppermute(block, "row", perm)


def send_col(block, pair, step):
    perm = [(a * 4 + z, (a ^ pair) * 4 + (z + step) % 4) for a in range(2) for z in range(4)]
    return lax.ppermute(block, "col", perm)


def swap_core(block):
    return lax.ppermute(block, "row", [(i, i ^ 1) for i in range(16)])


def gather(own, send):
    half = own.shape[0] // 2
    before, after, pair = send(own, 0, 1), send(own, 0, -1), send(own, 1, 0)
    low, high = send(before[:half], 0, 1), send(after[half:], 0, -1)
    pair_before, pair_after = send(pair, 0, 1), send(pair, 0, -1)
    opposite = jnp.concatenate([low, high], axis=0)
    pair_opposite = send(opposite, 1, 0)
    return {
        (0, 0): own, (0, 1): after, (0, 2): opposite, (0, 3): before,
        (1, 0): pair, (1, 1): pair_after, (1, 2): pair_opposite, (1, 3): pair_before,
    }


def wait_for(value, *others):
    return lax.optimization_barrier((value, *others))[0]


def scatter(part, send, first_work=None, last_work=None):
    sent = [part(1, 2).astype(BF), part(1, 1).astype(BF), part(1, 3).astype(BF)]
    far, from_before, from_after = send(sent[0], 1, 0), send(sent[1], 0, 1), send(sent[2], 0, -1)
    opposite = part(0, 2) + far.astype(F32)
    if first_work is not None:
        opposite = wait_for(opposite, first_work(lambda value: wait_for(value, *sent)))
    half = opposite.shape[0] // 2
    low = send(opposite[:half].astype(BF), 0, 1)
    high = send(opposite[half:].astype(BF), 0, -1)
    pair = (part(1, 0) + from_before.astype(F32) + from_after.astype(F32)).astype(BF)
    up, down = part(0, 1), part(0, 3)
    up = jnp.concatenate([up[:half] + low.astype(F32), up[half:]], axis=0).astype(BF)
    down = jnp.concatenate([down[:half], down[half:] + high.astype(F32)], axis=0).astype(BF)
    if last_work is not None:
        last_work(lambda value: wait_for(value, pair, up, down))
    pair, before, after = send(pair, 1, 0), send(up, 0, 1), send(down, 0, -1)
    return part(0, 0) + pair.astype(F32) + before.astype(F32) + after.astype(F32)


ORDER = [(b, k) for b in range(2) for k in range(4)]


def column_part(mine, other, rows):
    a, z = lax.axis_index("col") // 4, lax.axis_index("col") % 4

    def part(pair, step):
        at = ((z + step) % 4) * rows
        return jnp.where(
            (a ^ pair) == 0,
            lax.dynamic_slice_in_dim(mine, at, rows, 0),
            lax.dynamic_slice_in_dim(other, at, rows, 0),
        )

    return part


def column_panel(pieces):
    a, z = lax.axis_index("col") // 4, lax.axis_index("col") % 4
    rows, width = pieces[0, 0].shape
    panel = jnp.zeros((8 * rows, width), BF)
    for (pair, step), piece in pieces.items():
        at = ((a ^ pair) * 4 + (z + step) % 4) * rows
        panel = lax.dynamic_update_slice_in_dim(panel, piece, at, 0)
    return panel


def chip_sum(half_term):
    other = swap_core(half_term(1).astype(BF))
    return half_term(0) + other.astype(F32)


def body(tokens, in_weight, in_bias, out_weight, out_bias, out_grad):
    rows = tokens.shape[0]
    half = 8 * rows

    pieces = gather(jnp.concatenate([tokens, out_grad], axis=0), send_row)
    tok_mine = jnp.concatenate([pieces[s][:rows] for s in ORDER], axis=0)
    grad_mine = jnp.concatenate([pieces[s][rows:] for s in ORDER], axis=0)
    tok_mine, grad_mine = lax.optimization_barrier((tok_mine, grad_mine))
    tok_other = swap_core(tok_mine)
    grad_other = swap_core(grad_mine)

    hidden_part = column_part(matmul(tok_mine, in_weight), matmul(tok_other, in_weight), 2 * rows)
    pre_act = scatter(hidden_part, send_col) + in_bias
    grad_act_part = column_part(
        contract_last(grad_mine, out_weight), contract_last(grad_other, out_weight), 2 * rows
    )
    act = gelu_tanh(pre_act).astype(BF)
    act_all = column_panel(gather(act, send_col))
    grad_act = scatter(grad_act_part, send_col)
    _, pull_back = jax.vjp(gelu_tanh, pre_act)
    grad_pre = pull_back(grad_act)[0].astype(BF)
    grad_pre_all = column_panel(gather(grad_pre, send_col))

    output_mine = chip_sum(lambda d: matmul(act_all[d * half:(d + 1) * half], out_weight))
    grad_tokens_mine = chip_sum(
        lambda d: contract_last(grad_pre_all[d * half:(d + 1) * half], in_weight)
    )

    def row_part(pair, step):
        at = ORDER.index((pair, step % 4)) * rows
        return jnp.concatenate([output_mine[at:at + rows], grad_tokens_mine[at:at + rows]], axis=0)

    results = {}

    def output_weight(held):
        grad_all = held(jnp.concatenate([grad_mine, grad_other], axis=0))
        results["grad_out_weight"] = contract_first(act_all, grad_all)
        results["grad_out_bias"] = jnp.sum(grad_all, axis=0, dtype=F32)
        return results["grad_out_weight"]

    def input_weight(held):
        tok_all = held(jnp.concatenate([tok_mine, tok_other], axis=0))
        results["grad_in_weight"] = contract_first(tok_all, grad_pre_all).astype(BF)
        results["grad_in_bias"] = jnp.sum(grad_pre_all, axis=0, dtype=F32)

    both = scatter(row_part, send_row, output_weight, input_weight)
    output, grad_tokens = both[:rows] + out_bias, both[rows:]
    return (
        output, grad_tokens, results["grad_in_weight"], results["grad_in_bias"],
        results["grad_out_weight"], results["grad_out_bias"],
    )


def solution(mesh):
    in_specs = (
        P("row", "col"),
        P("col", "row"),
        P("row"),
        P("row", "col"),
        P("col"),
        P("row", "col"),
    )
    out_specs = (
        P("row", "col"),
        P("row", "col"),
        P("col", "row"),
        P("row"),
        P("row", "col"),
        P("col"),
    )
    return jax.shard_map(body, mesh=mesh, in_specs=in_specs, out_specs=out_specs, check_vma=False)
```

```python
import jax
import jax.numpy as jnp
from jax import lax
from jax.experimental import pallas as pl
from jax.experimental.pallas import tpu as pltpu
from jax.sharding import PartitionSpec as P

BF = jnp.bfloat16
F32 = jnp.float32


def gelu_tanh(value):
    return jax.nn.gelu(value, approximate=True)


def contract_last(left, right):
    return lax.dot_general(left, right, (((1,), (1,)), ((), ())), preferred_element_type=F32)


def contract_first(left, right):
    return lax.dot_general(left, right, (((0,), (0,)), ((), ())), preferred_element_type=F32)


def matmul(left, right):
    return jnp.dot(left, right, preferred_element_type=F32)


def row_index(hi, y, core):
    return (hi * 4 + y) * 2 + core


def send_row(block, pair, step):
    perm = [
        (row_index(h, y, c), row_index(h ^ pair, (y + step) % 4, c))
        for h in range(2) for y in range(4) for c in range(2)
    ]
    return lax.ppermute(block, "row", perm)


def send_col(block, pair, step):
    perm = [(a * 4 + z, (a ^ pair) * 4 + (z + step) % 4) for a in range(2) for z in range(4)]
    return lax.ppermute(block, "col", perm)


def swap_core(block):
    return lax.ppermute(block, "row", [(i, i ^ 1) for i in range(16)])


def gather(own, send):
    half = own.shape[0] // 2
    before, after, pair = send(own, 0, 1), send(own, 0, -1), send(own, 1, 0)
    low, high = send(before[:half], 0, 1), send(after[half:], 0, -1)
    pair_before, pair_after = send(pair, 0, 1), send(pair, 0, -1)
    opposite = jnp.concatenate([low, high], axis=0)
    pair_opposite = send(opposite, 1, 0)
    return {
        (0, 0): own, (0, 1): after, (0, 2): opposite, (0, 3): before,
        (1, 0): pair, (1, 1): pair_after, (1, 2): pair_opposite, (1, 3): pair_before,
    }


def wait_for(value, *others):
    return lax.optimization_barrier((value, *others))[0]


def scatter(part, send):
    far = send(part(1, 2).astype(BF), 1, 0)
    from_before, from_after = send(part(1, 1).astype(BF), 0, 1), send(part(1, 3).astype(BF), 0, -1)
    opposite = part(0, 2) + far.astype(F32)
    half = opposite.shape[0] // 2
    low = send(opposite[:half].astype(BF), 0, 1)
    high = send(opposite[half:].astype(BF), 0, -1)
    pair = send((part(1, 0) + from_before.astype(F32) + from_after.astype(F32)).astype(BF), 1, 0)
    up, down = part(0, 1), part(0, 3)
    up = jnp.concatenate([up[:half] + low.astype(F32), up[half:]], axis=0)
    down = jnp.concatenate([down[:half], down[half:] + high.astype(F32)], axis=0)
    before, after = send(up.astype(BF), 0, 1), send(down.astype(BF), 0, -1)
    return part(0, 0) + pair.astype(F32) + before.astype(F32) + after.astype(F32)


def gather_short(own, send):
    pair, before, after = send(own, 1, 0), send(own, 0, 1), send(own, 0, -1)
    opposite = send(own, 0, 2)
    pair_before, pair_after = send(pair, 0, 1), send(pair, 0, -1)
    pair_opposite = send(opposite, 1, 0)
    return {
        (0, 0): own, (0, 1): after, (0, 2): opposite, (0, 3): before,
        (1, 0): pair, (1, 1): pair_after, (1, 2): pair_opposite, (1, 3): pair_before,
    }


def scatter_short(part, send, first_work, last_work):
    sent = [part(*at).astype(BF) for at in ((1, 2), (1, 1), (1, 3), (0, 1), (0, 3))]
    far = send(sent[0], 1, 0)
    from_before, from_after = send(sent[1], 0, 1), send(sent[2], 0, -1)
    before, after = send(sent[3], 0, 1), send(sent[4], 0, -1)
    done = first_work(lambda value: wait_for(value, *sent))
    opposite = wait_for((part(0, 2) + far.astype(F32)).astype(BF), done)
    pair = (part(1, 0) + from_before.astype(F32) + from_after.astype(F32)).astype(BF)
    last_work(lambda value: wait_for(value, opposite, pair))
    opposite, pair = send(opposite, 0, 2), send(pair, 1, 0)
    total = part(0, 0) + before.astype(F32) + after.astype(F32)
    return total + opposite.astype(F32) + pair.astype(F32)


ORDER = [(b, k) for b in range(2) for k in range(4)]


def column_part(mine, other, rows):
    a, z = lax.axis_index("col") // 4, lax.axis_index("col") % 4

    def part(pair, step):
        at = ((z + step) % 4) * rows
        return jnp.where(
            (a ^ pair) == 0,
            lax.dynamic_slice_in_dim(mine, at, rows, 0),
            lax.dynamic_slice_in_dim(other, at, rows, 0),
        )

    return part


def copy_all(pairs, sems):
    copies = [pltpu.make_async_copy(src, dst, sems.at[i]) for i, (src, dst) in enumerate(pairs)]
    for copy in copies:
        copy.start()
    for copy in copies:
        copy.wait()


def column_panel(pieces, hold=None):
    rows, width = pieces[0, 0].shape
    n = len(ORDER)
    held = [] if hold is None else [hold]

    def kernel(*refs):
        out, sems = refs[-2:]
        a, z = lax.axis_index("col") // 4, lax.axis_index("col") % 4
        pairs = []
        for i, (pair, step) in enumerate(ORDER):
            at = ((a ^ pair) * 4 + (z + step) % 4) * rows
            pairs.append((refs[i], out.at[pl.ds(pl.multiple_of(at, rows), rows)]))
        copy_all(pairs, sems)

    return pl.pallas_call(
        kernel,
        out_shape=pltpu.VMEM((n * rows, width), BF),
        in_specs=[pl.BlockSpec(memory_space=pl.ANY)] * (n + len(held)),
        out_specs=pl.BlockSpec(memory_space=pltpu.VMEM),
        scratch_shapes=[pltpu.SemaphoreType.DMA((n,))],
        compiler_params=pltpu.CompilerParams(vmem_limit_bytes=1 << 20),
        name="column_panel",
    )(*[pieces[s] for s in ORDER], *held)


def body(tokens, in_weight, in_bias, out_weight, out_bias, out_grad):
    rows = tokens.shape[0]
    half = 8 * rows

    stacked = lax.optimization_barrier(jnp.concatenate([tokens, out_grad], axis=0))
    pieces = gather_short(stacked, send_row)
    tok_mine = jnp.concatenate([pieces[s][:rows] for s in ORDER], axis=0)
    grad_mine = jnp.concatenate([pieces[s][rows:] for s in ORDER], axis=0)
    tok_mine, grad_mine = lax.optimization_barrier((tok_mine, grad_mine))
    tok_other = swap_core(tok_mine)
    grad_other = swap_core(grad_mine)

    hidden_part = column_part(matmul(tok_mine, in_weight), matmul(tok_other, in_weight), 2 * rows)
    pre_act = scatter(hidden_part, send_col) + in_bias
    grad_act_part = column_part(
        contract_last(wait_for(grad_mine, hidden_part(1, 2).astype(BF)), out_weight),
        contract_last(grad_other, out_weight),
        2 * rows,
    )
    act = gelu_tanh(pre_act).astype(BF)
    act_all = column_panel(gather(act, send_col))
    grad_act = scatter(grad_act_part, send_col)
    _, pull_back = jax.vjp(gelu_tanh, pre_act)
    grad_pre = pull_back(grad_act)[0].astype(BF)

    output_sent = matmul(act_all[half:], out_weight).astype(BF)
    grad_pre_all = column_panel(gather(grad_pre, send_col), output_sent)
    grad_tokens_sent = contract_last(grad_pre_all[half:], in_weight).astype(BF)
    output_sent = wait_for(output_sent, grad_tokens_sent)
    output_mine = matmul(act_all[:half], out_weight) + swap_core(output_sent).astype(F32)
    grad_tokens_mine = contract_last(grad_pre_all[:half], in_weight)
    grad_tokens_mine = grad_tokens_mine + swap_core(grad_tokens_sent).astype(F32)

    def row_part(pair, step):
        at = ORDER.index((pair, step % 4)) * rows
        return jnp.concatenate([output_mine[at:at + rows], grad_tokens_mine[at:at + rows]], axis=0)

    results = {}

    def output_weight(held):
        grad_all = jnp.concatenate([held(grad_mine), held(grad_other)], axis=0)
        results["grad_out_weight"] = contract_first(act_all, grad_all)
        results["grad_out_bias"] = jnp.sum(grad_all, axis=0, dtype=F32)
        return results["grad_out_weight"]

    def input_weight(held):
        tok_all = jnp.concatenate([held(tok_mine), held(tok_other)], axis=0)
        results["grad_in_weight"] = contract_first(tok_all, grad_pre_all).astype(BF)
        results["grad_in_bias"] = jnp.sum(grad_pre_all, axis=0, dtype=F32)

    both = scatter_short(row_part, send_row, output_weight, input_weight)
    output, grad_tokens = both[:rows] + out_bias, both[rows:]
    return (
        output, grad_tokens, results["grad_in_weight"], results["grad_in_bias"],
        results["grad_out_weight"], results["grad_out_bias"],
    )


def solution(mesh):
    in_specs = (
        P("row", "col"),
        P("col", "row"),
        P("row"),
        P("row", "col"),
        P("col"),
        P("row", "col"),
    )
    out_specs = (
        P("row", "col"),
        P("row", "col"),
        P("col", "row"),
        P("row"),
        P("row", "col"),
        P("col"),
    )
    return jax.shard_map(body, mesh=mesh, in_specs=in_specs, out_specs=out_specs, check_vma=False)
```

```python
import jax
import jax.numpy as jnp
from jax import lax
from jax.experimental import pallas as pl
from jax.experimental.pallas import tpu as pltpu
from jax.sharding import PartitionSpec as P

BF = jnp.bfloat16
F32 = jnp.float32


def gelu_tanh(value):
    return jax.nn.gelu(value, approximate=True)


def contract_last(left, right):
    return lax.dot_general(left, right, (((1,), (1,)), ((), ())), preferred_element_type=F32)


def contract_first(left, right):
    return lax.dot_general(left, right, (((0,), (0,)), ((), ())), preferred_element_type=F32)


def matmul(left, right):
    return jnp.dot(left, right, preferred_element_type=F32)


def row_index(hi, y, core):
    return (hi * 4 + y) * 2 + core


def send_row(block, pair, step):
    perm = [
        (row_index(h, y, c), row_index(h ^ pair, (y + step) % 4, c))
        for h in range(2) for y in range(4) for c in range(2)
    ]
    return lax.ppermute(block, "row", perm)


def send_col(block, pair, step):
    perm = [(a * 4 + z, (a ^ pair) * 4 + (z + step) % 4) for a in range(2) for z in range(4)]
    return lax.ppermute(block, "col", perm)


def swap_core(block):
    return lax.ppermute(block, "row", [(i, i ^ 1) for i in range(16)])


def gather(own, send):
    half = own.shape[0] // 2
    before, after, pair = send(own, 0, 1), send(own, 0, -1), send(own, 1, 0)
    low, high = send(before[:half], 0, 1), send(after[half:], 0, -1)
    pair_before, pair_after = send(pair, 0, 1), send(pair, 0, -1)
    opposite = jnp.concatenate([low, high], axis=0)
    pair_opposite = send(opposite, 1, 0)
    return {
        (0, 0): own, (0, 1): after, (0, 2): opposite, (0, 3): before,
        (1, 0): pair, (1, 1): pair_after, (1, 2): pair_opposite, (1, 3): pair_before,
    }


def wait_for(value, *others):
    return lax.optimization_barrier((value, *others))[0]


def scatter(part, send):
    far = send(part(1, 2).astype(BF), 1, 0)
    from_before, from_after = send(part(1, 1).astype(BF), 0, 1), send(part(1, 3).astype(BF), 0, -1)
    opposite = part(0, 2) + far.astype(F32)
    half = opposite.shape[0] // 2
    low = send(opposite[:half].astype(BF), 0, 1)
    high = send(opposite[half:].astype(BF), 0, -1)
    pair = send((part(1, 0) + from_before.astype(F32) + from_after.astype(F32)).astype(BF), 1, 0)
    up, down = part(0, 1), part(0, 3)
    up = jnp.concatenate([up[:half] + low.astype(F32), up[half:]], axis=0)
    down = jnp.concatenate([down[:half], down[half:] + high.astype(F32)], axis=0)
    before, after = send(up.astype(BF), 0, 1), send(down.astype(BF), 0, -1)
    return part(0, 0) + pair.astype(F32) + before.astype(F32) + after.astype(F32)


def gather_short(own, send):
    pair, before, after = send(own, 1, 0), send(own, 0, 1), send(own, 0, -1)
    opposite = send(own, 0, 2)
    pair_before, pair_after = send(pair, 0, 1), send(pair, 0, -1)
    pair_opposite = send(opposite, 1, 0)
    return {
        (0, 0): own, (0, 1): after, (0, 2): opposite, (0, 3): before,
        (1, 0): pair, (1, 1): pair_after, (1, 2): pair_opposite, (1, 3): pair_before,
    }


def scatter_short(part, send, first_work, last_work):
    sent = [part(*at).astype(BF) for at in ((1, 2), (1, 1), (1, 3), (0, 1), (0, 3))]
    far = send(sent[0], 1, 0)
    from_before, from_after = send(sent[1], 0, 1), send(sent[2], 0, -1)
    before, after = send(sent[3], 0, 1), send(sent[4], 0, -1)
    done = first_work(lambda value: wait_for(value, *sent))
    opposite = wait_for((part(0, 2) + far.astype(F32)).astype(BF), done)
    pair = (part(1, 0) + from_before.astype(F32) + from_after.astype(F32)).astype(BF)
    last_work(lambda value: wait_for(value, opposite, pair))
    opposite, pair = send(opposite, 0, 2), send(pair, 1, 0)
    total = part(0, 0) + before.astype(F32) + after.astype(F32)
    return total + opposite.astype(F32) + pair.astype(F32)


ORDER = [(b, k) for b in range(2) for k in range(4)]


def column_part(mine, other, rows):
    a, z = lax.axis_index("col") // 4, lax.axis_index("col") % 4

    def part(pair, step):
        at = ((z + step) % 4) * rows
        return jnp.where(
            (a ^ pair) == 0,
            lax.dynamic_slice_in_dim(mine, at, rows, 0),
            lax.dynamic_slice_in_dim(other, at, rows, 0),
        )

    return part


def copy_all(pairs, sems):
    copies = [pltpu.make_async_copy(src, dst, sems.at[i]) for i, (src, dst) in enumerate(pairs)]
    for copy in copies:
        copy.start()
    for copy in copies:
        copy.wait()


def column_panel(pieces, *held):
    rows, width = pieces[0, 0].shape
    n = len(ORDER)

    def kernel(*refs):
        out, sems = refs[-2:]
        a, z = lax.axis_index("col") // 4, lax.axis_index("col") % 4
        pairs = []
        for i, (pair, step) in enumerate(ORDER):
            at = ((a ^ pair) * 4 + (z + step) % 4) * rows
            pairs.append((refs[i], out.at[pl.ds(pl.multiple_of(at, rows), rows)]))
        copy_all(pairs, sems)

    return pl.pallas_call(
        kernel,
        out_shape=pltpu.VMEM((n * rows, width), BF),
        in_specs=[pl.BlockSpec(memory_space=pl.ANY)] * (n + len(held)),
        out_specs=pl.BlockSpec(memory_space=pltpu.VMEM),
        scratch_shapes=[pltpu.SemaphoreType.DMA((n,))],
        compiler_params=pltpu.CompilerParams(vmem_limit_bytes=1 << 20),
        name="column_panel",
    )(*[pieces[s] for s in ORDER], *held)


def body(tokens, in_weight, in_bias, out_weight, out_bias, out_grad):
    rows = tokens.shape[0]
    half = 8 * rows

    stacked = lax.optimization_barrier(jnp.concatenate([tokens, out_grad], axis=0))
    pieces = gather_short(stacked, send_row)
    tok_mine = jnp.concatenate([pieces[s][:rows] for s in ORDER], axis=0)
    grad_mine = jnp.concatenate([pieces[s][rows:] for s in ORDER], axis=0)
    tok_mine, grad_mine = lax.optimization_barrier((tok_mine, grad_mine))
    tok_other = swap_core(tok_mine)
    grad_other = swap_core(grad_mine)

    hidden_part = column_part(matmul(tok_mine, in_weight), matmul(tok_other, in_weight), 2 * rows)
    pre_act = scatter(hidden_part, send_col) + in_bias
    grad_act_part = column_part(
        contract_last(wait_for(grad_mine, hidden_part(1, 2).astype(BF)), out_weight),
        contract_last(grad_other, out_weight),
        2 * rows,
    )
    act = gelu_tanh(pre_act).astype(BF)
    act_all = column_panel(gather(act, send_col))
    grad_act = scatter(grad_act_part, send_col)
    _, pull_back = jax.vjp(gelu_tanh, pre_act)
    grad_pre = pull_back(grad_act)[0].astype(BF)

    output_sent = matmul(act_all[half:], out_weight).astype(BF)
    output_kept = lax.optimization_barrier(matmul(act_all[:half], out_weight))
    grad_pre_all = column_panel(gather(grad_pre, send_col), output_sent)
    grad_tokens_sent = contract_last(grad_pre_all[half:], in_weight).astype(BF)
    grad_tokens_kept = lax.optimization_barrier(contract_last(grad_pre_all[:half], in_weight))
    output_mine = output_kept + swap_core(wait_for(output_sent, grad_tokens_sent)).astype(F32)
    grad_tokens_mine = grad_tokens_kept + swap_core(grad_tokens_sent).astype(F32)

    def row_part(pair, step):
        at = ORDER.index((pair, step % 4)) * rows
        return jnp.concatenate([output_mine[at:at + rows], grad_tokens_mine[at:at + rows]], axis=0)

    results = {}

    def output_weight(held):
        grad_all = jnp.concatenate([held(grad_mine), held(grad_other)], axis=0)
        results["grad_out_weight"] = contract_first(act_all, grad_all)
        return results["grad_out_weight"]

    def input_weight(held):
        tok_all = jnp.concatenate([held(tok_mine), held(tok_other)], axis=0)
        results["grad_in_weight"] = contract_first(tok_all, grad_pre_all).astype(BF)
        results["grad_in_bias"] = jnp.sum(grad_pre_all, axis=0, dtype=F32)
        grad_sums = [jnp.sum(held(x), axis=0, dtype=F32) for x in (grad_mine, grad_other)]
        results["grad_out_bias"] = grad_sums[0] + grad_sums[1]

    both = scatter_short(row_part, send_row, output_weight, input_weight)
    output, grad_tokens = both[:rows] + out_bias, both[rows:]
    return (
        output, grad_tokens, results["grad_in_weight"], results["grad_in_bias"],
        results["grad_out_weight"], results["grad_out_bias"],
    )


def solution(mesh):
    in_specs = (
        P("row", "col"),
        P("col", "row"),
        P("row"),
        P("row", "col"),
        P("col"),
        P("row", "col"),
    )
    out_specs = (
        P("row", "col"),
        P("row", "col"),
        P("col", "row"),
        P("row"),
        P("row", "col"),
        P("col"),
    )
    return jax.shard_map(body, mesh=mesh, in_specs=in_specs, out_specs=out_specs, check_vma=False)
```

```python
import jax
import jax.numpy as jnp
from jax import lax
from jax.experimental import pallas as pl
from jax.experimental.pallas import tpu as pltpu
from jax.sharding import PartitionSpec as P

BF = jnp.bfloat16
F32 = jnp.float32


def gelu_tanh(value):
    return jax.nn.gelu(value, approximate=True)


def contract_last(left, right):
    return lax.dot_general(left, right, (((1,), (1,)), ((), ())), preferred_element_type=F32)


def contract_first(left, right):
    return lax.dot_general(left, right, (((0,), (0,)), ((), ())), preferred_element_type=F32)


def matmul(left, right):
    return jnp.dot(left, right, preferred_element_type=F32)


def row_index(hi, y, core):
    return (hi * 4 + y) * 2 + core


def send_row(block, pair, step):
    perm = [
        (row_index(h, y, c), row_index(h ^ pair, (y + step) % 4, c))
        for h in range(2) for y in range(4) for c in range(2)
    ]
    return lax.ppermute(block, "row", perm)


def send_col(block, pair, step):
    perm = [(a * 4 + z, (a ^ pair) * 4 + (z + step) % 4) for a in range(2) for z in range(4)]
    return lax.ppermute(block, "col", perm)


def swap_core(block):
    return lax.ppermute(block, "row", [(i, i ^ 1) for i in range(16)])


def gather(own, send):
    half = own.shape[0] // 2
    before, after, pair = send(own, 0, 1), send(own, 0, -1), send(own, 1, 0)
    low, high = send(before[:half], 0, 1), send(after[half:], 0, -1)
    pair_before, pair_after = send(pair, 0, 1), send(pair, 0, -1)
    opposite = jnp.concatenate([low, high], axis=0)
    pair_opposite = send(opposite, 1, 0)
    return {
        (0, 0): own, (0, 1): after, (0, 2): opposite, (0, 3): before,
        (1, 0): pair, (1, 1): pair_after, (1, 2): pair_opposite, (1, 3): pair_before,
    }


def wait_for(value, *others):
    return lax.optimization_barrier((value, *others))[0]


def scatter(part, send):
    far = send(part(1, 2).astype(BF), 1, 0)
    from_before, from_after = send(part(1, 1).astype(BF), 0, 1), send(part(1, 3).astype(BF), 0, -1)
    opposite = part(0, 2) + far.astype(F32)
    half = opposite.shape[0] // 2
    low = send(opposite[:half].astype(BF), 0, 1)
    high = send(opposite[half:].astype(BF), 0, -1)
    pair = send((part(1, 0) + from_before.astype(F32) + from_after.astype(F32)).astype(BF), 1, 0)
    up, down = part(0, 1), part(0, 3)
    up = jnp.concatenate([up[:half] + low.astype(F32), up[half:]], axis=0)
    down = jnp.concatenate([down[:half], down[half:] + high.astype(F32)], axis=0)
    before, after = send(up.astype(BF), 0, 1), send(down.astype(BF), 0, -1)
    return part(0, 0) + pair.astype(F32) + before.astype(F32) + after.astype(F32)


def gather_short(own, send):
    pair, before, after = send(own, 1, 0), send(own, 0, 1), send(own, 0, -1)
    opposite = send(own, 0, 2)
    pair_before, pair_after = send(pair, 0, 1), send(pair, 0, -1)
    pair_opposite = send(opposite, 1, 0)
    return {
        (0, 0): own, (0, 1): after, (0, 2): opposite, (0, 3): before,
        (1, 0): pair, (1, 1): pair_after, (1, 2): pair_opposite, (1, 3): pair_before,
    }


def scatter_short(part, send, first_work, last_work):
    sent = [part(*at).astype(BF) for at in ((1, 2), (1, 1), (1, 3), (0, 1), (0, 3))]
    far = send(sent[0], 1, 0)
    from_before, from_after = send(sent[1], 0, 1), send(sent[2], 0, -1)
    before, after = send(sent[3], 0, 1), send(sent[4], 0, -1)
    done = first_work(lambda value: wait_for(value, *sent))
    opposite = wait_for((part(0, 2) + far.astype(F32)).astype(BF), done)
    pair = (part(1, 0) + from_before.astype(F32) + from_after.astype(F32)).astype(BF)
    last_work(lambda value: wait_for(value, opposite, pair))
    opposite, pair = send(opposite, 0, 2), send(pair, 1, 0)
    total = part(0, 0) + before.astype(F32) + after.astype(F32)
    return total + opposite.astype(F32) + pair.astype(F32)


ORDER = [(b, k) for b in range(2) for k in range(4)]


def column_part(mine, other, rows):
    a, z = lax.axis_index("col") // 4, lax.axis_index("col") % 4

    def part(pair, step):
        at = ((z + step) % 4) * rows
        return jnp.where(
            (a ^ pair) == 0,
            lax.dynamic_slice_in_dim(mine, at, rows, 0),
            lax.dynamic_slice_in_dim(other, at, rows, 0),
        )

    return part


def copy_all(pairs, sems):
    copies = [pltpu.make_async_copy(src, dst, sems.at[i]) for i, (src, dst) in enumerate(pairs)]
    for copy in copies:
        copy.start()
    for copy in copies:
        copy.wait()


def column_panel(pieces, *held):
    rows, width = pieces[0, 0].shape
    n = len(ORDER)

    def kernel(*refs):
        out, sems = refs[-2:]
        a, z = lax.axis_index("col") // 4, lax.axis_index("col") % 4
        pairs = []
        for i, (pair, step) in enumerate(ORDER):
            at = ((a ^ pair) * 4 + (z + step) % 4) * rows
            pairs.append((refs[i], out.at[pl.ds(pl.multiple_of(at, rows), rows)]))
        copy_all(pairs, sems)

    return pl.pallas_call(
        kernel,
        out_shape=pltpu.VMEM((n * rows, width), BF),
        in_specs=[pl.BlockSpec(memory_space=pl.ANY)] * (n + len(held)),
        out_specs=pl.BlockSpec(memory_space=pltpu.VMEM),
        scratch_shapes=[pltpu.SemaphoreType.DMA((n,))],
        compiler_params=pltpu.CompilerParams(vmem_limit_bytes=1 << 20),
        name="column_panel",
    )(*[pieces[s] for s in ORDER], *held)


def body(tokens, in_weight, in_bias, out_weight, out_bias, out_grad):
    rows = tokens.shape[0]
    half = 8 * rows

    stacked = lax.optimization_barrier(jnp.concatenate([tokens, out_grad], axis=0))
    pieces = gather_short(stacked, send_row)
    tok_mine = jnp.concatenate([pieces[s][:rows] for s in ORDER], axis=0)
    grad_mine = jnp.concatenate([pieces[s][rows:] for s in ORDER], axis=0)
    tok_mine, grad_mine = lax.optimization_barrier((tok_mine, grad_mine))
    tok_other = swap_core(tok_mine)
    grad_other = swap_core(grad_mine)

    hidden_part = column_part(matmul(tok_mine, in_weight), matmul(tok_other, in_weight), 2 * rows)
    pre_act = scatter(hidden_part, send_col) + in_bias
    grad_act_part = column_part(
        contract_last(wait_for(grad_mine, hidden_part(1, 2).astype(BF)), out_weight),
        contract_last(grad_other, out_weight),
        2 * rows,
    )
    act = gelu_tanh(pre_act).astype(BF)
    act_all = column_panel(gather(act, send_col))
    grad_act = scatter(grad_act_part, send_col)
    _, pull_back = jax.vjp(gelu_tanh, pre_act)
    grad_pre = pull_back(grad_act)[0].astype(BF)
    bias_part = jnp.sum(grad_pre, axis=0, dtype=F32, keepdims=True)
    bias_parts = lax.all_gather(bias_part, "col", axis=0, tiled=True)

    output_sent = matmul(act_all[half:], out_weight).astype(BF)
    output_kept = lax.optimization_barrier(matmul(act_all[:half], out_weight))
    grad_pre_all = column_panel(gather(grad_pre, send_col), output_sent)
    grad_tokens_sent = contract_last(grad_pre_all[half:], in_weight).astype(BF)
    grad_tokens_kept = lax.optimization_barrier(contract_last(grad_pre_all[:half], in_weight))
    output_mine = output_kept + swap_core(wait_for(output_sent, grad_tokens_sent)).astype(F32)
    grad_tokens_mine = grad_tokens_kept + swap_core(grad_tokens_sent).astype(F32)

    def row_part(pair, step):
        at = ORDER.index((pair, step % 4)) * rows
        return jnp.concatenate([output_mine[at:at + rows], grad_tokens_mine[at:at + rows]], axis=0)

    results = {}

    def output_weight(held):
        grad_all = jnp.concatenate([held(grad_mine), held(grad_other)], axis=0)
        results["grad_out_weight"] = contract_first(act_all, grad_all)
        return results["grad_out_weight"]

    def input_weight(held):
        tok_all = jnp.concatenate([held(tok_mine), held(tok_other)], axis=0)
        results["grad_in_weight"] = contract_first(tok_all, grad_pre_all).astype(BF)
        grad_sums = [jnp.sum(held(x), axis=0, dtype=F32) for x in (grad_mine, grad_other)]
        results["grad_out_bias"] = grad_sums[0] + grad_sums[1]

    both = scatter_short(row_part, send_row, output_weight, input_weight)
    output, grad_tokens = both[:rows] + out_bias, both[rows:]
    return (
        output, grad_tokens, results["grad_in_weight"], jnp.sum(bias_parts, axis=0),
        results["grad_out_weight"], results["grad_out_bias"],
    )


def solution(mesh):
    in_specs = (
        P("row", "col"),
        P("col", "row"),
        P("row"),
        P("row", "col"),
        P("col"),
        P("row", "col"),
    )
    out_specs = (
        P("row", "col"),
        P("row", "col"),
        P("col", "row"),
        P("row"),
        P("row", "col"),
        P("col"),
    )
    return jax.shard_map(body, mesh=mesh, in_specs=in_specs, out_specs=out_specs, check_vma=False)
```
